256 devices in a mesh: seq: 16 (over z, y_hi), res: 16 (over y_lo, x, core).
Axes of the slice: x: 4, y: 4 (y_hi: 2, y_lo: 2; y = y_hi * 2 + y_lo), z: 8, core: 2. Of those that a mesh axis runs over, the one named last changes fastest.
Arguments:
- homolog_profile: bfloat16 [128, 2048, 256], P('seq', 'res'), may hold values from -6 to 6
- couplings_tensor: bfloat16 [2048, 2048, 128], P('res', 'seq'), may hold values from -6 to 6
- present_entries: int32 [128, 2048], P('seq', 'res'), may hold values 0 or 1
- resolved_positions: int32 [2048], P('res'), may hold values 0 or 1
- coupling_logit_matrix: bfloat16 [128, 8], replicated
- horizontal_asking_matrix: bfloat16 [256, 256], replicated
- horizontal_lookup_matrix: bfloat16 [256, 256], replicated, may hold values from -0.375 to 0.375
- horizontal_content_matrix: bfloat16 [256, 256], replicated, may hold values from -0.375 to 0.375
- horizontal_sigmoid_matrix: bfloat16 [256, 256], replicated, may hold values from -0.375 to 0.375
- horizontal_final_matrix: bfloat16 [256, 256], replicated, may hold values from -0.375 to 0.375
- vertical_asking_matrix: bfloat16 [256, 256], replicated
- vertical_lookup_matrix: bfloat16 [256, 256], replicated, may hold values from -0.375 to 0.375
- vertical_content_matrix: bfloat16 [256, 256], replicated, may hold values from -0.375 to 0.375
- vertical_sigmoid_matrix: bfloat16 [256, 256], replicated, may hold values from -0.375 to 0.375
- vertical_final_matrix: bfloat16 [256, 256], replicated, may hold values from -0.375 to 0.375
- widening_matrix: bfloat16 [256, 1024], replicated, may hold values from -0.375 to 0.375
- narrowing_matrix: bfloat16 [1024, 256], replicated, may hold values from -0.1875 to 0.1875
Outputs:
- msa_next: bfloat16 [128, 2048, 256], P('seq', 'res')
The draws below stay inside these ranges and needn't reach their ends.
All inputs are finite; a program needn't handle non-finite values. No bound on the sum of `present_entries` or of `resolved_positions` on one device may be relied on, other than what follows from the above.
Results may differ from the reference program's by a relative error of at most 0.014.
The reference program's roundings to bfloat16 on the way count: a program that leaves them out, or rounds other values in their place, can miss the bound.
Values may be sent and summed in bfloat16 or wider, within the bound.
No kernel may reach another device: no remote copies, remote signals or barrier semaphores. Data moves between devices by JAX's collectives and lax.ppermute only.
A program may use at most 128 MiB of HBM per device.

```python
import jax
import jax.numpy as jnp
from jax import lax

HEADS = 8
HEAD_DIM = 32
CZ = 128
WIDEN_FACTOR = 4
EMBED_DEPTH = 256
HOMOLOG_NUMBER = 128
CHAIN_POSITIONS = 2048
N_RES = 16


def draw_coupling_logit_matrix(key, part):
    key = jax.random.fold_in(key, 11)
    starting_offset = jax.random.truncated_normal(key, -4.0, 4.0, (CZ, HEADS), jnp.float32) * (3.0 * CZ ** (-0.5))
    return starting_offset.astype(jnp.bfloat16)


def draw_horizontal_asking_matrix(key, part):
    key = jax.random.fold_in(key, 12)
    starting_offset = jax.random.truncated_normal(key, -4.0, 4.0, (EMBED_DEPTH, EMBED_DEPTH), jnp.float32) * EMBED_DEPTH ** (-0.5)
    return starting_offset.astype(jnp.bfloat16)


def draw_vertical_asking_matrix(key, part):
    key = jax.random.fold_in(key, 13)
    starting_offset = jax.random.truncated_normal(key, -4.0, 4.0, (EMBED_DEPTH, EMBED_DEPTH), jnp.float32) * EMBED_DEPTH ** (-0.5)
    return starting_offset.astype(jnp.bfloat16)


def plant(entries, stream_key, low, high):
    shape = entries.shape
    spot = [jax.random.randint(jax.random.fold_in(stream_key, axis), (), 0, shape[axis]) for axis in range(len(shape))]
    entries = entries.at[tuple(spot)].set(low)
    longest = shape.index(max(shape))
    spot[longest] = (spot[longest] + 1) % shape[longest]
    return entries.at[tuple(spot)].set(high)


def level_of(own_key, shape, pieces, smallest, largest):
    def one(position, blocks):
        draws = jax.random.uniform(jax.random.fold_in(jax.random.fold_in(own_key, 6), position), (blocks,), jnp.float32, smallest / len(pieces), largest / len(pieces))
        return jnp.repeat(jnp.exp(draws), shape[position] // blocks).reshape((-1,) + (1,) * (len(shape) - position - 1))

    loudness = one(*pieces[0])
    for cut in pieces[1:]:
        loudness = loudness * one(*cut)
    return loudness


def scatter_about(key, extent, scale, most, shards=(), kind=jnp.bfloat16):
    gain = level_of(key, extent, shards, -0.22, 0.18) if shards else 1.0
    array = jax.random.normal(key, extent, jnp.float32) * scale * gain
    return jnp.minimum(jnp.maximum(array, -most), most).astype(kind)


def setup_inputs(seed: int = 0) -> dict:
    splits = jax.random.split(jax.random.key(seed), 18)
    return {
        "homolog_profile": scatter_about(splits[0], (HOMOLOG_NUMBER, CHAIN_POSITIONS, EMBED_DEPTH), 1.0, 6.0, ((0, 16), (1, 16))),
        "couplings_tensor": scatter_about(splits[1], (CHAIN_POSITIONS, CHAIN_POSITIONS, CZ), 1.0, 6.0, ((0, 16), (1, 16))),
        "present_entries": plant((jax.random.randint(splits[2], (HOMOLOG_NUMBER, CHAIN_POSITIONS), 0, 8) < 7).astype(jnp.int32), jax.random.fold_in(splits[2], 1), 0, 1),
        "resolved_positions": plant((jax.random.randint(splits[3], (CHAIN_POSITIONS,), 0, 16) < 15).astype(jnp.int32), jax.random.fold_in(splits[3], 1), 0, 1),
        "coupling_logit_matrix": draw_coupling_logit_matrix(jax.random.fold_in(splits[17], 71), 0),
        "horizontal_asking_matrix": draw_horizontal_asking_matrix(jax.random.fold_in(splits[17], 71), 0),
        "horizontal_lookup_matrix": scatter_about(splits[6], (EMBED_DEPTH, EMBED_DEPTH), EMBED_DEPTH ** -0.5, 0.375),
        "horizontal_content_matrix": scatter_about(splits[7], (EMBED_DEPTH, EMBED_DEPTH), EMBED_DEPTH ** -0.5, 0.375),
        "horizontal_sigmoid_matrix": scatter_about(splits[8], (EMBED_DEPTH, EMBED_DEPTH), EMBED_DEPTH ** -0.5, 0.375),
        "horizontal_final_matrix": scatter_about(splits[9], (EMBED_DEPTH, EMBED_DEPTH), EMBED_DEPTH ** -0.5, 0.375),
        "vertical_asking_matrix": draw_vertical_asking_matrix(jax.random.fold_in(splits[17], 71), 0),
        "vertical_lookup_matrix": scatter_about(splits[11], (EMBED_DEPTH, EMBED_DEPTH), EMBED_DEPTH ** -0.5, 0.375),
        "vertical_content_matrix": scatter_about(splits[12], (EMBED_DEPTH, EMBED_DEPTH), EMBED_DEPTH ** -0.5, 0.375),
        "vertical_sigmoid_matrix": scatter_about(splits[13], (EMBED_DEPTH, EMBED_DEPTH), EMBED_DEPTH ** -0.5, 0.375),
        "vertical_final_matrix": scatter_about(splits[14], (EMBED_DEPTH, EMBED_DEPTH), EMBED_DEPTH ** -0.5, 0.375),
        "widening_matrix": scatter_about(splits[15], (EMBED_DEPTH, WIDEN_FACTOR * EMBED_DEPTH), EMBED_DEPTH ** -0.5, 0.375),
        "narrowing_matrix": scatter_about(splits[16], (WIDEN_FACTOR * EMBED_DEPTH, EMBED_DEPTH), (WIDEN_FACTOR * EMBED_DEPTH) ** -0.5, 0.1875),
    }


EPS = 1e-05
MASK_SCALE = 1000000000.0

def standardize_features_fn(values):
    values = values.astype(jnp.float32)
    center = values - lax.optimization_barrier(jnp.mean(values, -1, keepdims=True))
    spread = lax.optimization_barrier(jnp.mean(center * center, -1, keepdims=True))
    return center * lax.rsqrt(spread + EPS)

def bias_rows(block, coupling_logit_matrix):
    return jnp.einsum('ijc,ch->hij', standardize_features_fn(block), coupling_logit_matrix.astype(jnp.float32), precision=lax.Precision.HIGHEST).astype(jnp.bfloat16)

def rounded_weights(probs):
    low = lax.optimization_barrier(probs.astype(jnp.bfloat16))
    return low.astype(jnp.float32)

def column_block(inputs, okay, w_query, w_key, w_value, w_gate):
    number_entries, homolog_groups, embedding_depth = inputs.shape
    head_dim = embedding_depth // HEADS
    scale = HEAD_DIM ** (-0.5)
    query = (jnp.dot(inputs, w_query, preferred_element_type=jnp.float32) * scale).astype(jnp.bfloat16)
    keys = jnp.dot(inputs, w_key, preferred_element_type=jnp.float32).astype(jnp.bfloat16)
    values = jnp.dot(inputs, w_value, preferred_element_type=jnp.float32).astype(jnp.bfloat16)
    gate = jax.nn.sigmoid(jnp.dot(inputs, w_gate, preferred_element_type=jnp.float32))
    query = query.reshape(number_entries, homolog_groups, HEADS, head_dim).astype(jnp.float32)
    keys = keys.reshape(number_entries, homolog_groups, HEADS, head_dim).astype(jnp.float32)
    values = values.reshape(number_entries, homolog_groups, HEADS, head_dim).astype(jnp.float32)
    masking = ((okay.astype(jnp.float32) - 1.0) * MASK_SCALE).T
    score = jnp.einsum('sihd,tihd->ihst', query, keys) + masking[:, None, None, :]
    probs = jnp.exp(score - lax.optimization_barrier(jnp.max(score, -1, keepdims=True)))
    total = lax.optimization_barrier(jnp.sum(probs, -1))
    mixed = jnp.einsum('ihst,tihd->sihd', rounded_weights(probs), values)
    mixed = mixed / jnp.transpose(total, (2, 0, 1))[..., None]
    return (mixed.reshape(number_entries, homolog_groups, embedding_depth) * gate).astype(jnp.bfloat16)

def reference(homolog_profile, couplings_tensor, present_entries, resolved_positions, coupling_logit_matrix, horizontal_asking_matrix, horizontal_lookup_matrix, horizontal_content_matrix, horizontal_sigmoid_matrix, horizontal_final_matrix, vertical_asking_matrix, vertical_lookup_matrix, vertical_content_matrix, vertical_sigmoid_matrix, vertical_final_matrix, widening_matrix, narrowing_matrix):
    number_entries, stretch_extent, embedding_depth = homolog_profile.shape
    head_dim = embedding_depth // HEADS
    scale = HEAD_DIM ** (-0.5)
    blocks = couplings_tensor.reshape(N_RES, stretch_extent // N_RES, stretch_extent, CZ)
    bias = lax.map(lambda block: bias_rows(block, coupling_logit_matrix), blocks)
    bias = jnp.transpose(bias, (1, 0, 2, 3)).reshape(HEADS, stretch_extent, stretch_extent)
    lone_source_tensor = standardize_features_fn(homolog_profile).astype(jnp.bfloat16)
    query = (jnp.dot(lone_source_tensor, horizontal_asking_matrix, preferred_element_type=jnp.float32) * scale).astype(jnp.bfloat16)
    keys = jnp.dot(lone_source_tensor, horizontal_lookup_matrix, preferred_element_type=jnp.float32).astype(jnp.bfloat16)
    values = jnp.dot(lone_source_tensor, horizontal_content_matrix, preferred_element_type=jnp.float32).astype(jnp.bfloat16)
    gate = jax.nn.sigmoid(jnp.dot(lone_source_tensor, horizontal_sigmoid_matrix, preferred_element_type=jnp.float32))
    key_valid = present_entries * resolved_positions[None, :]

    def row_one(items):
        qq, kk, vv, ok = items
        qq = qq.reshape(stretch_extent, HEADS, head_dim).astype(jnp.float32)
        kk = kk.reshape(stretch_extent, HEADS, head_dim).astype(jnp.float32)
        vv = vv.reshape(stretch_extent, HEADS, head_dim).astype(jnp.float32)
        score = jnp.einsum('ihd,jhd->hij', qq, kk) + bias.astype(jnp.float32)
        score = score + ((ok.astype(jnp.float32) - 1.0) * MASK_SCALE)[None, None, :]
        probs = jnp.exp(score - lax.optimization_barrier(jnp.max(score, -1, keepdims=True)))
        total = lax.optimization_barrier(jnp.sum(probs, -1))
        mixed = jnp.einsum('hij,jhd->ihd', rounded_weights(probs), vv)
        mixed = mixed / jnp.transpose(total)[..., None]
        return mixed.reshape(stretch_extent, embedding_depth)
    row_mixed = lax.map(row_one, (query, keys, values, key_valid))
    lone_head_mixing = (row_mixed * gate).astype(jnp.bfloat16)
    lone_homolog_group = homolog_profile.astype(jnp.float32) + jnp.dot(lone_head_mixing, horizontal_final_matrix, preferred_element_type=jnp.float32)
    second_activations = standardize_features_fn(lone_homolog_group).astype(jnp.bfloat16)
    split_parts = stretch_extent // N_RES
    x_blocks = jnp.moveaxis(second_activations.reshape(number_entries, N_RES, split_parts, embedding_depth), 1, 0)
    valid_blocks = jnp.moveaxis(present_entries.reshape(number_entries, N_RES, split_parts), 1, 0)
    second_mixing = lax.map(lambda items: column_block(items[0], items[1], vertical_asking_matrix, vertical_lookup_matrix, vertical_content_matrix, vertical_sigmoid_matrix), (x_blocks, valid_blocks))
    second_mixing = jnp.moveaxis(second_mixing, 0, 1).reshape(number_entries, stretch_extent, embedding_depth)
    updated_profile = lone_homolog_group + jnp.dot(second_mixing, vertical_final_matrix, preferred_element_type=jnp.float32)
    x_three = standardize_features_fn(updated_profile).astype(jnp.bfloat16)
    hidden = jax.nn.relu(jnp.dot(x_three, widening_matrix, preferred_element_type=jnp.float32)).astype(jnp.bfloat16)
    return (updated_profile + jnp.dot(hidden, narrowing_matrix, preferred_element_type=jnp.float32)).astype(jnp.bfloat16)
```

```python
import functools

import jax
import jax.numpy as jnp
import numpy as np
from jax import lax
from jax.experimental import pallas as pl
from jax.experimental.pallas import tpu as pltpu
from jax.sharding import PartitionSpec as P

HEADS = 8
HEAD_DIM = 32
EPS = 1e-05
MASK_SCALE = 1000000000.0
VMEM_LIMIT = 48 * 1024 * 1024

F32 = jnp.float32
BF16 = jnp.bfloat16


def mask_parts():
    parts = []
    rest = np.float64(-MASK_SCALE)
    for _ in range(3):
        part = np.float64(np.asarray(rest, jnp.bfloat16))
        parts.append(float(part))
        rest = rest - part
    assert rest == 0.0
    return parts


def standardize(values):
    center = values - jnp.mean(values, -1, keepdims=True)
    spread = jnp.mean(center * center, -1, keepdims=True)
    return center * lax.rsqrt(spread + EPS)


def dot_tt(a, b):
    return lax.dot_general(a, b, (((0,), (1,)), ((), ())), preferred_element_type=F32)


def dot_tn(a, b):
    return lax.dot_general(a, b, (((0,), (0,)), ((), ())), preferred_element_type=F32)


def dot_nt(a, b):
    return lax.dot_general(a, b, (((1,), (1,)), ((), ())), preferred_element_type=F32)


def dot_nn(a, b):
    return lax.dot_general(a, b, (((1,), (0,)), ((), ())), preferred_element_type=F32)


def whole(*_):
    return pl.BlockSpec(memory_space=pltpu.VMEM)


def params(**kw):
    return pltpu.CompilerParams(vmem_limit_bytes=VMEM_LIMIT, **kw)


def cost(us):
    return pl.CostEstimate(flops=int(us * 1e-6 * 9e14), bytes_accessed=1024, transcendentals=0)


def tokens_kernel(hp_ref, ok_ref, wq_ref, wk_ref, wv_ref, wg_ref, send_ref, gate_ref):
    x = standardize(hp_ref[...].reshape(1024, 256).astype(F32)).astype(BF16)
    scale = HEAD_DIM ** (-0.5)
    for n, w_ref in enumerate((wq_ref, wk_ref, wv_ref)):
        t = dot_tt(w_ref[...], x)
        if n == 0:
            t = t * scale
        t = t.astype(BF16)
        for h in range(HEADS):
            for s in range(8):
                send_ref[h, n * 256 + s * 32 : n * 256 + (s + 1) * 32, :] = t[
                    h * 32 : (h + 1) * 32, s * 128 : (s + 1) * 128
                ]
    ok = jnp.concatenate([ok_ref[...], jnp.zeros((8, 128), F32)], 0).astype(BF16)
    for h in range(HEADS):
        send_ref[h, 768:784, :] = ok
    gate_ref[...] = jax.nn.sigmoid(dot_tt(wg_ref[...], x))


def tokens_call(hp, ok, wq, wk, wv, wg):
    return pl.pallas_call(
        tokens_kernel,
        out_shape=(
            jax.ShapeDtypeStruct((8, 784, 128), BF16),
            jax.ShapeDtypeStruct((256, 1024), F32),
        ),
        in_specs=[whole()] * 6,
        out_specs=(whole(), whole()),
        compiler_params=params(),
        cost_estimate=cost(5),
        name="tokens",
    )(hp, ok, wq, wk, wv, wg)


BIAS_ROWS = 16


def bias_kernel(z_ref, wt_ref, out_ref, rows):
    step = pl.program_id(0)
    wt = wt_ref[...]
    ones_row = jnp.ones((16, 128), BF16)
    wsum = jnp.sum(wt.astype(F32), -1, keepdims=True)
    for n in range(BIAS_ROWS):
        z = z_ref[n]
        zf = z.astype(F32)
        center = zf - jnp.mean(zf, -1, keepdims=True)
        square = center * center
        high = square.astype(BF16)
        low = (square - high.astype(F32)).astype(BF16)
        dots = dot_nt(wt, z)
        mean = dot_nt(ones_row, z)[0:8] * (1.0 / 128)
        spread = (dot_nt(ones_row, high) + dot_nt(ones_row, low))[0:8] * (1.0 / 128)
        res = (dots[0:8] - mean * wsum[0:8]) * lax.rsqrt(spread + EPS)
        rows[pl.ds(step * BIAS_ROWS + n, 8, stride=128), :] = res

    @pl.when(step == pl.num_programs(0) - 1)
    def _():
        for h in range(HEADS):
            out_ref[h] = rows[h * 128 : (h + 1) * 128, :].T.astype(BF16)


def bias_call(z, wt):
    return pl.pallas_call(
        bias_kernel,
        out_shape=jax.ShapeDtypeStruct((8, 128, 128), BF16),
        grid=(128 // BIAS_ROWS,),
        in_specs=[
            pl.BlockSpec((BIAS_ROWS, 128, 128), lambda n: (n, 0, 0)),
            pl.BlockSpec((16, 128), lambda n: (0, 0)),
        ],
        out_specs=pl.BlockSpec((8, 128, 128), lambda n: (0, 0, 0)),
        scratch_shapes=[pltpu.VMEM((1024, 128), F32)],
        compiler_params=params(),
        cost_estimate=cost(8),
        name="pair_bias",
    )(z, wt)


def attend_kernel(n_bias, chunks, first, last, *refs):
    place_ref, own_ref, other_ref = refs[:3]
    bias_refs = refs[3 : 3 + n_bias]
    refs = refs[3 + n_bias :]
    if not first:
        m_in, l_in, acc_in = refs[:3]
        refs = refs[3:]
    if last:
        o_ref = refs[0]
        refs = refs[1:]
    else:
        m_ref, l_ref, acc_ref = refs[:3]
        refs = refs[3:]
    keys, vals = refs
    z = place_ref[0]
    slot_own = place_ref[1]
    parts = mask_parts()
    rowid = lax.broadcasted_iota(jnp.int32, (16, 128), 0)
    coeff = jnp.where(rowid == 0, parts[0], jnp.where(rowid == 1, parts[1], jnp.where(rowid == 2, parts[2], 0.0)))
    rowid = lax.broadcasted_iota(jnp.int32, (16, 256), 0)
    ones = jnp.where(rowid < 3, 1.0, 0.0).astype(BF16)
    n_chunks = len(chunks)

    for c, (shift, _) in enumerate(chunks):
        zz = lax.rem(z + shift + 8, 8)
        for src, slot in ((own_ref, slot_own), (other_ref, 1 - slot_own)):
            okay = src[zz, 768:784, :].astype(F32)
            for s in range(8):
                mask = ((1.0 - okay[s : s + 1, :]) * coeff).astype(BF16)
                kt = jnp.concatenate([src[zz, 256 + s * 32 : 256 + (s + 1) * 32, :], mask], 0)
                keys[c, slot, s] = kt.T
                vals[c, slot, s] = src[zz, 512 + s * 32 : 512 + (s + 1) * 32, :]

    def one_sequence(s, carry):
        kx = jnp.concatenate([keys[c, t, s] for c in range(n_chunks) for t in range(2)], 0)
        vt = jnp.concatenate([vals[c, t, s] for c in range(n_chunks) for t in range(2)], 1)
        for tile in range(4):
            lanes = slice(tile * 256, (tile + 1) * 256)
            q = jnp.concatenate(
                [own_ref[tile * 2 + u, pl.ds(pl.multiple_of(s * 32, 32), 32), :] for u in range(2)], 1
            )
            qx = jnp.concatenate([q, ones], 0)
            bias = jnp.concatenate(
                [
                    jnp.concatenate([bias_refs[b][t, tile * 2 + u] for u in range(2)], 1)
                    for _, slots in chunks
                    for b, t in slots
                ],
                0,
            )
            score = dot_nn(kx, qx) + bias.astype(F32)
            top = jnp.max(score, 0, keepdims=True)
            if not first:
                before = m_in[s, :, lanes]
                top = jnp.maximum(top, before)
            probs = jnp.exp(score - top)
            total = jnp.sum(probs, 0, keepdims=True)
            accum = dot_nn(vt, probs.astype(BF16))
            if not first:
                factor = jnp.exp(before - top)
                total = total + l_in[s, :, lanes] * factor
                accum = accum + acc_in[s, :, lanes] * factor
            if last:
                out = (accum / total).astype(BF16)
                for u in range(2):
                    o_ref[tile * 2 + u, pl.ds(pl.multiple_of(s * 32, 32), 32), :] = out[:, u * 128 : (u + 1) * 128]
            else:
                m_ref[s, :, lanes] = top
                l_ref[s, :, lanes] = total
                acc_ref[s, :, lanes] = accum
        return carry

    lax.fori_loop(0, 8, one_sequence, 0)


def attend_call(place, own, other, biases, chunks, state, last, us):
    first = state is None
    if last:
        out_shape = jax.ShapeDtypeStruct((8, 256, 128), BF16)
        out_specs = whole()
    else:
        out_shape = (
            jax.ShapeDtypeStruct((8, 1, 1024), F32),
            jax.ShapeDtypeStruct((8, 1, 1024), F32),
            jax.ShapeDtypeStruct((8, 32, 1024), F32),
        )
        out_specs = (whole(),) * 3
    args = [place, own, other, *biases] + ([] if first else list(state))
    return pl.pallas_call(
        functools.partial(attend_kernel, len(biases), chunks, first, last),
        out_shape=out_shape,
        in_specs=[pl.BlockSpec(memory_space=pltpu.SMEM)] + [whole()] * (len(args) - 1),
        out_specs=out_specs,
        scratch_shapes=[
            pltpu.VMEM((len(chunks), 2, 8, 128, 48), BF16),
            pltpu.VMEM((len(chunks), 2, 8, 32, 128), BF16),
        ],
        compiler_params=params(),
        cost_estimate=cost(us),
        name="attend",
    )(*args)


def mix_kernel(o_ref, gate_ref, hp_ref, present_ref, wf_ref, m1_ref, x2_ref):
    pieces = []
    wf = wf_ref[...]
    for s in range(8):
        ot = jnp.concatenate([o_ref[h, s * 32 : (s + 1) * 32, :] for h in range(HEADS)], 0)
        at = (ot.astype(F32) * gate_ref[:, s * 128 : (s + 1) * 128]).astype(BF16)
        m1 = hp_ref[s].astype(F32) + dot_tn(at, wf)
        m1_ref[s] = m1
        pieces.append(standardize(m1).reshape(16, 8, 256))
    present = present_ref[...]
    wide = jnp.concatenate([present, jnp.zeros_like(present)], 1)
    pieces.append(jnp.stack([pltpu.roll(wide, (256 - 8 * a) % 256, 1) for a in range(16)], 0))
    x2_ref[...] = jnp.concatenate(pieces, 1).astype(BF16)


def mix_call(o, gate, hp, present, wf):
    return pl.pallas_call(
        mix_kernel,
        out_shape=(
            jax.ShapeDtypeStruct((8, 128, 256), F32),
            jax.ShapeDtypeStruct((16, 72, 256), BF16),
        ),
        in_specs=[whole()] * 5,
        out_specs=(whole(), whole()),
        compiler_params=params(),
        cost_estimate=cost(5),
        name="row_mix",
    )(o, gate, hp, present, wf)


def column_kernel(x_ref, wq_ref, wk_ref, wv_ref, wg_ref, out_ref, rows0, rows1):
    x = x_ref[...].astype(F32)
    rows = (rows0, rows1)
    xs = x[:, :64, :].reshape(1024, 256)
    rows0[...] = xs[:, :128]
    rows1[...] = xs[:, 128:]
    masks = x[:, 64:72, :128].reshape(128, 128).T
    cols = jnp.concatenate(
        [jnp.concatenate([r[pl.ds(i, 128, stride=8), :] for r in rows], 1) for i in range(8)], 0
    ).astype(BF16)
    scale = HEAD_DIM ** (-0.5)
    qt = (dot_tt(wq_ref[...], cols) * scale).astype(BF16)
    kt = dot_tt(wk_ref[...], cols).astype(BF16)
    vt = dot_tt(wv_ref[...], cols).astype(BF16)
    gt = jax.nn.sigmoid(dot_tt(wg_ref[...], cols))
    parts = mask_parts()
    rowid = lax.broadcasted_iota(jnp.int32, (16, 128), 0)
    coeff = jnp.where(rowid == 0, parts[0], jnp.where(rowid == 1, parts[1], jnp.where(rowid == 2, parts[2], 0.0)))
    ones = jnp.where(rowid < 3, 1.0, 0.0).astype(BF16)
    for i in range(8):
        lanes = slice(i * 128, (i + 1) * 128)
        mask = ((1.0 - masks[i : i + 1, :]) * coeff).astype(BF16)
        heads = []
        for h in range(HEADS):
            ch = slice(h * 32, (h + 1) * 32)
            kx = jnp.concatenate([kt[ch, lanes], mask], 0)
            qx = jnp.concatenate([qt[ch, lanes], ones], 0)
            score = dot_tn(kx, qx)
            probs = jnp.exp(score - jnp.max(score, 0, keepdims=True))
            total = jnp.sum(probs, 0, keepdims=True)
            heads.append(dot_nn(vt[ch, lanes], probs.astype(BF16)) / total)
        at = jnp.concatenate(heads, 0) * gt[:, lanes]
        an = at.T
        for k, r in enumerate(rows):
            r[pl.ds(i, 128, stride=8), :] = an[:, k * 128 : (k + 1) * 128]
    out_ref[...] = jnp.concatenate([r[...] for r in rows], 1).astype(BF16).reshape(16, 64, 256)


def column_call(x, wq, wk, wv, wg):
    return pl.pallas_call(
        column_kernel,
        out_shape=jax.ShapeDtypeStruct((16, 64, 256), BF16),
        in_specs=[whole()] * 5,
        out_specs=whole(),
        scratch_shapes=[pltpu.VMEM((1024, 128), F32)] * 2,
        compiler_params=params(),
        cost_estimate=cost(10),
        name="column",
    )(x, wq, wk, wv, wg)


def final_kernel(a_ref, m1_ref, wf_ref, ww_ref, wn_ref, out_ref):
    a = a_ref[...].astype(F32)
    wf = wf_ref[...]
    ww = ww_ref[...]
    wn = wn_ref[...]
    for s in range(8):
        a2 = a[:, s * 8 : (s + 1) * 8, :].reshape(128, 256).astype(BF16)
        m2 = m1_ref[s] + dot_nn(a2, wf)
        x3 = standardize(m2).astype(BF16)
        hid = jnp.maximum(dot_nn(x3, ww), 0.0).astype(BF16)
        out_ref[s] = (m2 + dot_nn(hid, wn)).astype(BF16)


def final_call(a, m1, wf, ww, wn):
    return pl.pallas_call(
        final_kernel,
        out_shape=jax.ShapeDtypeStruct((8, 128, 256), BF16),
        in_specs=[whole()] * 5,
        out_specs=whole(),
        compiler_params=params(),
        cost_estimate=cost(6),
        name="transition",
    )(a, m1, wf, ww, wn)


def on_device(
    homolog_profile,
    couplings_tensor,
    present_entries,
    resolved_positions,
    coupling_logit_matrix,
    horizontal_asking_matrix,
    horizontal_lookup_matrix,
    horizontal_content_matrix,
    horizontal_sigmoid_matrix,
    horizontal_final_matrix,
    vertical_asking_matrix,
    vertical_lookup_matrix,
    vertical_content_matrix,
    vertical_sigmoid_matrix,
    vertical_final_matrix,
    widening_matrix,
    narrowing_matrix,
):
    seq = lax.axis_index("seq")
    res = lax.axis_index("res")
    same_core = [[r for r in range(16) if r % 2 == c] for c in range(2)]
    to_right = [(a, (a + 2) % 16) for a in range(16)]
    to_left = [(a, (a - 2) % 16) for a in range(16)]
    swap = [(a, a ^ 1) for a in range(16)]

    def to_heads(x):
        return lax.all_to_all(x, "res", 0, 0, axis_index_groups=same_core, tiled=True)

    present = present_entries.astype(F32)
    okay = (present_entries * resolved_positions[None, :]).astype(F32)
    wt = jnp.zeros((16, 128), BF16).at[:8].set(coupling_logit_matrix.T)
    place = jnp.stack([seq // 2, jnp.where(res % 2 == seq % 2, 0, 1)]).astype(jnp.int32)

    send, gate = tokens_call(
        homolog_profile,
        okay,
        horizontal_asking_matrix,
        horizontal_lookup_matrix,
        horizontal_content_matrix,
        horizontal_sigmoid_matrix,
    )
    own = to_heads(send)
    other = lax.ppermute(own, "res", swap)

    bias = to_heads(bias_call(couplings_tensor, wt))
    pair = jnp.stack([bias, lax.ppermute(bias, "seq", swap)])

    state = attend_call(place, own, other, [pair], [(0, [(0, 0), (0, 1)])], None, False, 6)
    right, left = pair, pair
    for k in range(1, 4):
        right = lax.ppermute(right, "seq", to_right)
        left = lax.ppermute(left, "seq", to_left)
        chunks = [(-k, [(0, 0), (0, 1)]), (k, [(1, 0), (1, 1)])]
        state = attend_call(place, own, other, [right, left], chunks, state, False, 12)
    right = lax.ppermute(right[:1], "seq", to_right)
    left = lax.ppermute(left[1:], "seq", to_left)
    o = attend_call(place, own, other, [right, left], [(4, [(0, 0), (1, 0)])], state, True, 6)

    o = to_heads(o)
    m1, x2 = mix_call(o, gate, homolog_profile, present, horizontal_final_matrix)
    x2 = lax.all_to_all(x2, "seq", 0, 0, tiled=True)
    a2 = column_call(
        x2, vertical_asking_matrix, vertical_lookup_matrix, vertical_content_matrix, vertical_sigmoid_matrix
    )
    a2 = lax.all_to_all(a2, "seq", 0, 0, tiled=True)
    return final_call(a2, m1, vertical_final_matrix, widening_matrix, narrowing_matrix)


def solution(mesh):
    placed = (
        P("seq", "res", None),
        P("res", "seq", None),
        P("seq", "res"),
        P("res"),
    ) + (P(),) * 13
    return jax.shard_map(
        on_device, mesh=mesh, in_specs=placed, out_specs=P("seq", "res", None), check_vma=False
    )
```

```python
import functools

import jax
import jax.numpy as jnp
import numpy as np
from jax import lax
from jax.experimental import pallas as pl
from jax.experimental.pallas import tpu as pltpu
from jax.sharding import PartitionSpec as P

HEADS = 8
HEAD_DIM = 32
EPS = 1e-05
MASK_SCALE = 1000000000.0

F32 = jnp.float32
BF16 = jnp.bfloat16


def mask_parts():
    parts = []
    rest = np.float64(-MASK_SCALE)
    for _ in range(3):
        part = np.float64(np.asarray(rest, jnp.bfloat16))
        parts.append(float(part))
        rest = rest - part
    assert rest == 0.0
    return parts


def standardize(values):
    center = values - jnp.mean(values, -1, keepdims=True)
    spread = jnp.mean(center * center, -1, keepdims=True)
    return center * lax.rsqrt(spread + EPS)


def dot_tt(a, b):
    return lax.dot_general(a, b, (((0,), (1,)), ((), ())), preferred_element_type=F32)


def dot_tn(a, b):
    return lax.dot_general(a, b, (((0,), (0,)), ((), ())), preferred_element_type=F32)


def dot_nt(a, b):
    return lax.dot_general(a, b, (((1,), (1,)), ((), ())), preferred_element_type=F32)


def dot_nn(a, b):
    return lax.dot_general(a, b, (((1,), (0,)), ((), ())), preferred_element_type=F32)


def whole(*_):
    return pl.BlockSpec(memory_space=pltpu.VMEM)


def params(mib=24):
    return pltpu.CompilerParams(vmem_limit_bytes=mib * 1024 * 1024)


def cost(us):
    return pl.CostEstimate(flops=int(us * 1e-6 * 9e14), bytes_accessed=1024, transcendentals=0)


def tokens_kernel(hp_ref, ok_ref, wq_ref, wk_ref, wv_ref, wg_ref, send_ref, gate_ref):
    x = standardize(hp_ref[...].reshape(1024, 256).astype(F32)).astype(BF16)
    scale = HEAD_DIM ** (-0.5)
    for n, w_ref in enumerate((wq_ref, wk_ref, wv_ref)):
        t = dot_tt(w_ref[...], x)
        if n == 0:
            t = t * scale
        t = t.astype(BF16)
        for h in range(HEADS):
            for s in range(8):
                send_ref[h, n * 256 + s * 32 : n * 256 + (s + 1) * 32, :] = t[
                    h * 32 : (h + 1) * 32, s * 128 : (s + 1) * 128
                ]
    ok = jnp.concatenate([ok_ref[...], jnp.zeros((8, 128), F32)], 0).astype(BF16)
    for h in range(HEADS):
        send_ref[h, 768:784, :] = ok
    gate_ref[...] = jax.nn.sigmoid(dot_tt(wg_ref[...], x))


def tokens_call(hp, ok, wq, wk, wv, wg):
    return pl.pallas_call(
        tokens_kernel,
        out_shape=(
            jax.ShapeDtypeStruct((8, 784, 128), BF16),
            jax.ShapeDtypeStruct((256, 1024), F32),
        ),
        in_specs=[whole()] * 6,
        out_specs=(whole(), whole()),
        compiler_params=params(),
        cost_estimate=cost(5),
        name="tokens",
    )(hp, ok, wq, wk, wv, wg)


BIAS_ROWS = 64


def bias_kernel(z_ref, w_ref, out_ref, rows):
    step = pl.program_id(0)
    w = w_ref[...].astype(F32)
    wsum = jnp.sum(w, -1, keepdims=True)
    wt = jnp.concatenate([w, jnp.zeros((8, 128), F32)], 0).astype(BF16)
    for n in range(BIAS_ROWS):
        zt = z_ref[n].T
        zf = zt.astype(F32)
        mean = jnp.sum(zf, 0, keepdims=True) * (1.0 / 128)
        center = zf - mean
        spread = jnp.sum(center * center, 0, keepdims=True) * (1.0 / 128)
        res = (dot_nn(wt, zt)[0:8] - mean * wsum) * lax.rsqrt(spread + EPS)
        rows[pl.ds(step * BIAS_ROWS + n, 8, stride=128), :] = res

    @pl.when(step == pl.num_programs(0) - 1)
    def _():
        for h in range(HEADS):
            block = rows[h * 128 : (h + 1) * 128, :].T.astype(BF16)
            out_ref[h] = block
            out_ref[HEADS + h] = block


def bias_call(z, w):
    return pl.pallas_call(
        bias_kernel,
        out_shape=jax.ShapeDtypeStruct((16, 128, 128), BF16),
        grid=(128 // BIAS_ROWS,),
        in_specs=[
            pl.BlockSpec((BIAS_ROWS, 128, 128), lambda n: (n, 0, 0)),
            pl.BlockSpec((8, 128), lambda n: (0, 0)),
        ],
        out_specs=pl.BlockSpec((16, 128, 128), lambda n: (0, 0, 0)),
        scratch_shapes=[pltpu.VMEM((1024, 128), F32)],
        compiler_params=params(60),
        cost_estimate=cost(6),
        name="pair_bias",
    )(z, w)


def attend_kernel(width, unroll, n_bias, blocks, has_other, first, last, *refs):
    place_ref, own_ref = refs[:2]
    refs = refs[2:]
    sources = [own_ref]
    if has_other:
        sources.append(refs[0])
        refs = refs[1:]
    bias_refs = refs[:n_bias]
    refs = refs[n_bias:]
    if not first:
        m_in, l_in, acc_in = refs[:3]
        refs = refs[3:]
    if last:
        o_ref, keys = refs
    else:
        m_ref, l_ref, acc_ref, keys = refs
    z = place_ref[0]
    core = place_ref[1]
    parts = mask_parts()
    rowid = lax.broadcasted_iota(jnp.int32, (16, 128), 0)
    coeff = jnp.where(rowid == 0, parts[0], jnp.where(rowid == 1, parts[1], jnp.where(rowid == 2, parts[2], 0.0)))
    rowid = lax.broadcasted_iota(jnp.int32, (16, width), 0)
    ones = jnp.where(rowid < 3, 1.0, 0.0).astype(BF16)
    places = [(sources[far], lax.rem(z + shift + 8, 8)) for shift, far, _ in blocks]

    for n, (src, zz) in enumerate(places):
        okay = src[zz, 768:784, :].astype(F32)
        for s in range(8):
            mask = ((1.0 - okay[s : s + 1, :]) * coeff).astype(BF16)
            keys[n, s] = jnp.concatenate([src[zz, 256 + s * 32 : 256 + (s + 1) * 32, :], mask], 0).T

    span = width // 128

    def bias_block(n, tile):
        _, far, operands = blocks[n]
        slot = 1 - core if far else core
        ref = bias_refs[operands[tile * width // 512]]
        base = tile * span if ref.shape[1] == 8 else tile * span % 4
        return jnp.concatenate([ref[slot, base + u] for u in range(span)], 1)

    def scores(s, tile):
        kx = jnp.concatenate([keys[n, s] for n in range(len(blocks))], 0)
        q = jnp.concatenate(
            [own_ref[tile * span + u, pl.ds(pl.multiple_of(s * 32, 32), 32), :] for u in range(span)], 1
        )
        qx = jnp.concatenate([q, ones], 0)
        bias = jnp.concatenate([bias_block(n, tile) for n in range(len(blocks))], 0)
        return dot_nn(kx, qx) + bias.astype(F32)

    def finish(s, tile, score):
        lanes = slice(tile * width, (tile + 1) * width)
        top = jnp.max(score, 0, keepdims=True)
        if not first:
            before = m_in[s, :, lanes]
            top = jnp.maximum(top, before)
        probs = jnp.exp(score - top)
        total = jnp.sum(probs, 0, keepdims=True)
        vt = jnp.concatenate(
            [src[zz, pl.ds(pl.multiple_of(512 + s * 32, 32), 32), :] for src, zz in places], 1
        )
        accum = dot_nn(vt, probs.astype(BF16))
        if not first:
            factor = jnp.exp(before - top)
            total = total + l_in[s, :, lanes] * factor
            accum = accum + acc_in[s, :, lanes] * factor
        if last:
            out = (accum / total).astype(o_ref.dtype)
            for u in range(span):
                o_ref[tile * span + u, pl.ds(pl.multiple_of(s * 32, 32), 32), :] = out[
                    :, u * 128 : (u + 1) * 128
                ]
        else:
            m_ref[s, :, lanes] = top
            l_ref[s, :, lanes] = total
            acc_ref[s, :, lanes] = accum

    def some_sequences(k, carry):
        items = [(k * unroll + d, tile) for d in range(unroll) for tile in range(1024 // width)]
        score = scores(*items[0])
        for n, item in enumerate(items):
            upcoming = scores(*items[n + 1]) if n + 1 < len(items) else None
            finish(*item, score)
            score = upcoming
        return carry

    lax.fori_loop(0, 8 // unroll, some_sequences, 0)


def attend_call(place, own, other, biases, blocks, state, last, us):
    first = state is None
    if last:
        out_shape = jax.ShapeDtypeStruct((8, 256, 128), F32)
        out_specs = whole()
    else:
        out_shape = (
            jax.ShapeDtypeStruct((8, 1, 1024), F32),
            jax.ShapeDtypeStruct((8, 1, 1024), F32),
            jax.ShapeDtypeStruct((8, 32, 1024), F32),
        )
        out_specs = (whole(),) * 3
    args = [place, own] + ([] if other is None else [other]) + list(biases) + ([] if first else list(state))
    unroll = 4 if len(blocks) <= 4 else 2
    return pl.pallas_call(
        functools.partial(attend_kernel, 512, unroll, len(biases), blocks, other is not None, first, last),
        out_shape=out_shape,
        in_specs=[pl.BlockSpec(memory_space=pltpu.SMEM)] + [whole()] * (len(args) - 1),
        out_specs=out_specs,
        scratch_shapes=[pltpu.VMEM((len(blocks), 8, 128, 48), BF16)],
        compiler_params=params(),
        cost_estimate=cost(us),
        name="attend",
    )(*args)


def mix_kernel(o_ref, gate_ref, hp_ref, present_ref, wf_ref, m1_ref, x2_ref):
    pieces = []
    wf = wf_ref[...]
    for s in range(8):
        ot = jnp.concatenate([o_ref[h, s * 32 : (s + 1) * 32, :] for h in range(HEADS)], 0)
        at = (ot.astype(F32) * gate_ref[:, s * 128 : (s + 1) * 128]).astype(BF16)
        m1 = hp_ref[s].astype(F32) + dot_tn(at, wf)
        m1_ref[s] = m1
        pieces.append(standardize(m1).reshape(16, 8, 256))
    present = present_ref[...]
    wide = jnp.concatenate([present, jnp.zeros_like(present)], 1)
    pieces.append(jnp.stack([pltpu.roll(wide, (256 - 8 * a) % 256, 1) for a in range(16)], 0))
    x2_ref[...] = jnp.concatenate(pieces, 1).astype(BF16)


def mix_call(o, gate, hp, present, wf):
    return pl.pallas_call(
        mix_kernel,
        out_shape=(
            jax.ShapeDtypeStruct((8, 128, 256), F32),
            jax.ShapeDtypeStruct((16, 72, 256), BF16),
        ),
        in_specs=[whole()] * 5,
        out_specs=(whole(), whole()),
        compiler_params=params(),
        cost_estimate=cost(5),
        name="row_mix",
    )(o, gate, hp, present, wf)


def column_kernel(x_ref, wq_ref, wk_ref, wv_ref, wg_ref, out_ref, rows0, rows1):
    x = x_ref[...].astype(F32)
    rows = (rows0, rows1)
    xs = x[:, :64, :].reshape(1024, 256)
    rows0[...] = xs[:, :128]
    rows1[...] = xs[:, 128:]
    masks = (x[:, 64:72, :128].reshape(128, 128) - 1.0) * MASK_SCALE
    cols = jnp.concatenate(
        [jnp.concatenate([r[pl.ds(i, 128, stride=8), :] for r in rows], 1) for i in range(8)], 0
    ).astype(BF16)
    scale = HEAD_DIM ** (-0.5)
    qt = (dot_tt(wq_ref[...], cols) * scale).astype(BF16)
    kn = dot_nn(cols, wk_ref[...]).astype(BF16)
    vt = dot_tt(wv_ref[...], cols).astype(BF16)
    gt = jax.nn.sigmoid(dot_tt(wg_ref[...], cols))

    def scores(i, pair):
        lanes = slice(i * 128, (i + 1) * 128)
        sides = []
        for h in (pair * 2, pair * 2 + 1):
            parts = [qt[h * 32 : (h + 1) * 32, lanes]]
            if h > 0:
                parts.insert(0, jnp.zeros((h * 32, 128), BF16))
            if h < HEADS - 1:
                parts.append(jnp.zeros(((HEADS - 1 - h) * 32, 128), BF16))
            sides.append(jnp.concatenate(parts, 0))
        q = jnp.concatenate(sides, 1)
        return dot_nn(kn[i * 128 : (i + 1) * 128, :], q) + masks[:, i : i + 1]

    def finish(i, pair, score):
        lanes = slice(i * 128, (i + 1) * 128)
        probs = jnp.exp(score - jnp.max(score, 0, keepdims=True))
        total = jnp.sum(probs, 0, keepdims=True)
        accum = dot_nn(vt[pair * 64 : (pair + 1) * 64, lanes], probs.astype(BF16)) / total
        return [accum[:32, :128], accum[32:, 128:]]

    items = [(i, pair) for i in range(8) for pair in range(HEADS // 2)]
    score = scores(*items[0])
    heads = []
    for n, (i, pair) in enumerate(items):
        upcoming = scores(*items[n + 1]) if n + 1 < len(items) else None
        heads += finish(i, pair, score)
        score = upcoming
        if pair == HEADS // 2 - 1:
            an = (jnp.concatenate(heads, 0) * gt[:, i * 128 : (i + 1) * 128]).T
            heads = []
            for k, r in enumerate(rows):
                r[pl.ds(i, 128, stride=8), :] = an[:, k * 128 : (k + 1) * 128]
    out_ref[...] = jnp.concatenate([r[...] for r in rows], 1).astype(BF16).reshape(16, 64, 256)


def column_call(x, wq, wk, wv, wg):
    return pl.pallas_call(
        column_kernel,
        out_shape=jax.ShapeDtypeStruct((16, 64, 256), BF16),
        in_specs=[whole()] * 5,
        out_specs=whole(),
        scratch_shapes=[pltpu.VMEM((1024, 128), F32)] * 2,
        compiler_params=params(),
        cost_estimate=cost(10),
        name="column",
    )(x, wq, wk, wv, wg)


def final_kernel(a_ref, m1_ref, wf_ref, ww_ref, wn_ref, out_ref):
    a = a_ref[...].astype(F32)
    wf = wf_ref[...]
    ww = ww_ref[...]
    wn = wn_ref[...]
    for p in range(2):
        a2 = jnp.concatenate(
            [a[:, s * 8 : (s + 1) * 8, :].reshape(128, 256) for s in range(p * 4, p * 4 + 4)], 0
        ).astype(BF16)
        m2 = m1_ref[p * 4 : p * 4 + 4].reshape(512, 256) + dot_nn(a2, wf)
        x3 = standardize(m2).astype(BF16)
        hid = jnp.maximum(dot_nn(x3, ww), 0.0).astype(BF16)
        out_ref[p * 4 : p * 4 + 4] = (m2 + dot_nn(hid, wn)).astype(BF16).reshape(4, 128, 256)


def final_call(a, m1, wf, ww, wn):
    return pl.pallas_call(
        final_kernel,
        out_shape=jax.ShapeDtypeStruct((8, 128, 256), BF16),
        in_specs=[whole()] * 5,
        out_specs=whole(),
        compiler_params=params(),
        cost_estimate=cost(6),
        name="transition",
    )(a, m1, wf, ww, wn)


def on_device(
    homolog_profile,
    couplings_tensor,
    present_entries,
    resolved_positions,
    coupling_logit_matrix,
    horizontal_asking_matrix,
    horizontal_lookup_matrix,
    horizontal_content_matrix,
    horizontal_sigmoid_matrix,
    horizontal_final_matrix,
    vertical_asking_matrix,
    vertical_lookup_matrix,
    vertical_content_matrix,
    vertical_sigmoid_matrix,
    vertical_final_matrix,
    widening_matrix,
    narrowing_matrix,
):
    seq = lax.axis_index("seq")
    res = lax.axis_index("res")
    same_core = [[r for r in range(16) if r % 2 == c] for c in range(2)]
    to_right = [(a, (a + 2) % 16) for a in range(16)]
    to_left = [(a, (a - 2) % 16) for a in range(16)]
    swap = [(a, a ^ 1) for a in range(16)]

    wide_groups = [
        [(z * 2 + y) * 16 + g * 2 + c for y in range(2) for g in range(8)] for z in range(8) for c in range(2)
    ]

    def to_heads(x):
        return lax.all_to_all(x, "res", 0, 0, axis_index_groups=same_core, tiled=True)

    present = present_entries.astype(F32)
    okay = (present_entries * resolved_positions[None, :]).astype(F32)
    place = jnp.stack([seq // 2, res % 2]).astype(jnp.int32)

    barrier = lax.optimization_barrier
    bias = bias_call(couplings_tensor, coupling_logit_matrix.T)
    pair = lax.all_to_all(bias, ("seq", "res"), 0, 0, axis_index_groups=wide_groups, tiled=True)
    pair = pair.reshape(2, 8, 128, 128)
    send, gate = tokens_call(
        homolog_profile,
        okay,
        horizontal_asking_matrix,
        horizontal_lookup_matrix,
        horizontal_content_matrix,
        horizontal_sigmoid_matrix,
    )

    pair, send = barrier((pair, send))

    def ring(right, left):
        return lax.ppermute(right, "seq", to_right), lax.ppermute(left, "seq", to_left)

    def steps(far, *counts):
        blocks = []
        for n, k in counts:
            blocks += [(k, far, (n, n))] if k == 0 else [(-k, far, (n, n)), (k, far, (n + 1, n + 1))]
        return blocks

    one = ring(pair, pair)
    own = to_heads(send)
    two = ring(*one)
    own, one = barrier((own, one))
    other = lax.ppermute(own, "res", swap)
    near = [pair, *one]
    state = attend_call(place, own, None, near, steps(0, (0, 0), (1, 1)), None, False, 6)
    other, state = barrier((other, state))
    state = attend_call(place, own, other, near, steps(1, (0, 0), (1, 1)), state, False, 6)
    two, state = barrier((two, state))
    three = ring(*two)
    state = attend_call(place, own, other, two, steps(0, (0, 2)) + steps(1, (0, 2)), state, False, 7)
    three, state = barrier((three, state))
    four = ring(three[0][:, :4], three[1][:, 4:])
    state = attend_call(place, own, other, three, steps(0, (0, 3)) + steps(1, (0, 3)), state, False, 7)
    o = attend_call(place, own, other, four, [(4, 0, (0, 1)), (4, 1, (0, 1))], state, True, 4)

    o = to_heads(o)
    m1, x2 = mix_call(o, gate, homolog_profile, present, horizontal_final_matrix)
    x2 = lax.all_to_all(x2, "seq", 0, 0, tiled=True)
    a2 = column_call(
        x2, vertical_asking_matrix, vertical_lookup_matrix, vertical_content_matrix, vertical_sigmoid_matrix
    )
    a2 = lax.all_to_all(a2, "seq", 0, 0, tiled=True)
    return final_call(a2, m1, vertical_final_matrix, widening_matrix, narrowing_matrix)


def solution(mesh):
    placed = (
        P("seq", "res", None),
        P("res", "seq", None),
        P("seq", "res"),
        P("res"),
    ) + (P(),) * 13
    return jax.shard_map(
        on_device, mesh=mesh, in_specs=placed, out_specs=P("seq", "res", None), check_vma=False
    )
```

```python
import functools

import jax
import jax.numpy as jnp
import numpy as np
from jax import lax
from jax.experimental import pallas as pl
from jax.experimental.pallas import tpu as pltpu
from jax.sharding import PartitionSpec as P

HEADS = 8
HEAD_DIM = 32
EPS = 1e-05
MASK_SCALE = 1000000000.0

F32 = jnp.float32
BF16 = jnp.bfloat16


def mask_parts():
    parts = []
    rest = np.float64(-MASK_SCALE)
    for _ in range(3):
        part = np.float64(np.asarray(rest, jnp.bfloat16))
        parts.append(float(part))
        rest = rest - part
    assert rest == 0.0
    return parts


def standardize(values):
    center = values - jnp.mean(values, -1, keepdims=True)
    spread = jnp.mean(center * center, -1, keepdims=True)
    return center * lax.rsqrt(spread + EPS)


def dot_tt(a, b):
    return lax.dot_general(a, b, (((0,), (1,)), ((), ())), preferred_element_type=F32)


def dot_tn(a, b):
    return lax.dot_general(a, b, (((0,), (0,)), ((), ())), preferred_element_type=F32)


def dot_nt(a, b):
    return lax.dot_general(a, b, (((1,), (1,)), ((), ())), preferred_element_type=F32)


def dot_nn(a, b):
    return lax.dot_general(a, b, (((1,), (0,)), ((), ())), preferred_element_type=F32)


def whole(*_):
    return pl.BlockSpec(memory_space=pltpu.VMEM)


def params(mib=24):
    return pltpu.CompilerParams(vmem_limit_bytes=mib * 1024 * 1024)


def cost(us):
    return pl.CostEstimate(flops=int(us * 1e-6 * 9e14), bytes_accessed=1024, transcendentals=0)


def tokens_kernel(hp_ref, ok_ref, wq_ref, wk_ref, wv_ref, wg_ref, send_ref, gate_ref):
    x = standardize(hp_ref[...].reshape(1024, 256).astype(F32)).astype(BF16)
    scale = HEAD_DIM ** (-0.5)
    for n, w_ref in enumerate((wq_ref, wk_ref, wv_ref)):
        t = dot_tt(w_ref[...], x)
        if n == 0:
            t = t * scale
        t = t.astype(BF16)
        for h in range(HEADS):
            for s in range(8):
                send_ref[h, n * 256 + s * 32 : n * 256 + (s + 1) * 32, :] = t[
                    h * 32 : (h + 1) * 32, s * 128 : (s + 1) * 128
                ]
    ok = jnp.concatenate([ok_ref[...], jnp.zeros((8, 128), F32)], 0).astype(BF16)
    for h in range(HEADS):
        send_ref[h, 768:784, :] = ok
    gate_ref[...] = jax.nn.sigmoid(dot_tt(wg_ref[...], x))


def tokens_call(hp, ok, wq, wk, wv, wg):
    return pl.pallas_call(
        tokens_kernel,
        out_shape=(
            jax.ShapeDtypeStruct((8, 784, 128), BF16),
            jax.ShapeDtypeStruct((256, 1024), F32),
        ),
        in_specs=[whole()] * 6,
        out_specs=(whole(), whole()),
        compiler_params=params(),
        cost_estimate=cost(5),
        name="tokens",
    )(hp, ok, wq, wk, wv, wg)


BIAS_ROWS = 64


def bias_kernel(z_ref, w_ref, out_ref, rows):
    step = pl.program_id(0)
    w = w_ref[...].astype(F32)
    wsum = jnp.sum(w, -1, keepdims=True)
    wt = jnp.concatenate([w, jnp.zeros((8, 128), F32)], 0).astype(BF16)
    for n in range(BIAS_ROWS):
        zt = z_ref[n].T
        zf = zt.astype(F32)
        mean = jnp.sum(zf, 0, keepdims=True) * (1.0 / 128)
        center = zf - mean
        spread = jnp.sum(center * center, 0, keepdims=True) * (1.0 / 128)
        res = (dot_nn(wt, zt)[0:8] - mean * wsum) * lax.rsqrt(spread + EPS)
        rows[pl.ds(step * BIAS_ROWS + n, 8, stride=128), :] = res

    @pl.when(step == pl.num_programs(0) - 1)
    def _():
        for h in range(HEADS):
            block = rows[h * 128 : (h + 1) * 128, :].T.astype(BF16)
            out_ref[h] = block
            out_ref[HEADS + h] = block


def bias_call(z, w):
    return pl.pallas_call(
        bias_kernel,
        out_shape=jax.ShapeDtypeStruct((16, 128, 128), BF16),
        grid=(128 // BIAS_ROWS,),
        in_specs=[
            pl.BlockSpec((BIAS_ROWS, 128, 128), lambda n: (n, 0, 0)),
            pl.BlockSpec((8, 128), lambda n: (0, 0)),
        ],
        out_specs=pl.BlockSpec((16, 128, 128), lambda n: (0, 0, 0)),
        scratch_shapes=[pltpu.VMEM((1024, 128), F32)],
        compiler_params=params(60),
        cost_estimate=cost(6),
        name="pair_bias",
    )(z, w)


def attend_kernel(width, unroll, n_bias, blocks, has_other, fetch, first, last, *refs):
    place_ref, own_ref = refs[:2]
    refs = refs[2:]
    if has_other:
        far_ref, refs = refs[0], refs[1:]
    bias_refs = refs[:n_bias]
    refs = refs[n_bias:]
    if not first:
        m_in, l_in, acc_in = refs[:3]
        refs = refs[3:]
    copy = None
    if fetch:
        other_ref, far_ref, sem = far_ref, refs[3], refs[5]
        refs = [*refs[:3], refs[4]]
        copy = pltpu.make_async_copy(other_ref.at[:, pl.ds(256, 528)], far_ref, sem)
        copy.start()
    if last:
        o_ref, keys = refs
    else:
        m_ref, l_ref, acc_ref, keys = refs
    z = place_ref[0]
    core = place_ref[1]
    parts = mask_parts()
    rowid = lax.broadcasted_iota(jnp.int32, (16, 128), 0)
    coeff = jnp.where(rowid == 0, parts[0], jnp.where(rowid == 1, parts[1], jnp.where(rowid == 2, parts[2], 0.0)))
    rowid = lax.broadcasted_iota(jnp.int32, (16, width), 0)
    ones = jnp.where(rowid < 3, 1.0, 0.0).astype(BF16)
    places = []
    for shift, far, _ in blocks:
        zz = lax.rem(z + shift + 8, 8)
        places.append((far_ref, zz, 0) if far else (own_ref, zz, 256))

    if copy is not None:
        copy.wait()
    for n, (src, at, base) in enumerate(places):
        okay = src[at, base + 512 : base + 528, :].astype(F32)
        for s in range(8):
            mask = ((1.0 - okay[s : s + 1, :]) * coeff).astype(BF16)
            keys[n, s] = jnp.concatenate([src[at, base + s * 32 : base + (s + 1) * 32, :], mask], 0).T

    span = width // 128

    def bias_block(n, tile):
        _, far, operands = blocks[n]
        slot = 1 - core if far else core
        ref = bias_refs[operands[tile * width // 512]]
        base = tile * span if ref.shape[1] == 8 else tile * span % 4
        return jnp.concatenate([ref[slot, base + u] for u in range(span)], 1)

    def scores(s, tile):
        kx = jnp.concatenate([keys[n, s] for n in range(len(blocks))], 0)
        q = jnp.concatenate(
            [own_ref[tile * span + u, pl.ds(pl.multiple_of(s * 32, 32), 32), :] for u in range(span)], 1
        )
        qx = jnp.concatenate([q, ones], 0)
        bias = jnp.concatenate([bias_block(n, tile) for n in range(len(blocks))], 0)
        return dot_nn(kx, qx) + bias.astype(F32)

    def finish(s, tile, score):
        lanes = slice(tile * width, (tile + 1) * width)
        top = jnp.max(score, 0, keepdims=True)
        if not first:
            before = m_in[s, :, lanes]
            top = jnp.maximum(top, before)
        probs = jnp.exp(score - top)
        total = jnp.sum(probs, 0, keepdims=True)
        vt = jnp.concatenate(
            [src[at, pl.ds(pl.multiple_of(base + 256 + s * 32, 32), 32), :] for src, at, base in places], 1
        )
        accum = dot_nn(vt, probs.astype(BF16))
        if not first:
            factor = jnp.exp(before - top)
            total = total + l_in[s, :, lanes] * factor
            accum = accum + acc_in[s, :, lanes] * factor
        if last:
            out = (accum / total).astype(o_ref.dtype)
            for u in range(span):
                o_ref[tile * span + u, pl.ds(pl.multiple_of(s * 32, 32), 32), :] = out[
                    :, u * 128 : (u + 1) * 128
                ]
        else:
            m_ref[s, :, lanes] = top
            l_ref[s, :, lanes] = total
            acc_ref[s, :, lanes] = accum

    def some_sequences(k, carry):
        items = [(k * unroll + d, tile) for d in range(unroll) for tile in range(1024 // width)]
        score = scores(*items[0])
        for n, item in enumerate(items):
            upcoming = scores(*items[n + 1]) if n + 1 < len(items) else None
            finish(*item, score)
            score = upcoming
        return carry

    lax.fori_loop(0, 8 // unroll, some_sequences, 0)


def attend_call(place, own, other, biases, blocks, state, last, us, fetch=False):
    first = state is None
    if last:
        out_shape = jax.ShapeDtypeStruct((8, 256, 128), F32)
        out_specs = whole()
    else:
        out_shape = (
            jax.ShapeDtypeStruct((8, 1, 1024), F32),
            jax.ShapeDtypeStruct((8, 1, 1024), F32),
            jax.ShapeDtypeStruct((8, 32, 1024), F32),
        )
        out_specs = (whole(),) * 3
    args = [place, own] + ([] if other is None else [other]) + list(biases) + ([] if first else list(state))
    in_specs = [pl.BlockSpec(memory_space=pltpu.SMEM)] + [whole()] * (len(args) - 1)
    scratch = [pltpu.VMEM((len(blocks), 8, 128, 48), BF16)]
    if fetch:
        in_specs[2] = pl.BlockSpec(memory_space=pl.ANY)
        out_shape += (jax.ShapeDtypeStruct((8, 528, 128), BF16),)
        out_specs += (whole(),)
        scratch.append(pltpu.SemaphoreType.DMA)
    unroll = 4 if len(blocks) <= 4 else 2
    return pl.pallas_call(
        functools.partial(attend_kernel, 512, unroll, len(biases), blocks, other is not None, fetch, first, last),
        out_shape=out_shape,
        in_specs=in_specs,
        out_specs=out_specs,
        scratch_shapes=scratch,
        compiler_params=params(),
        cost_estimate=cost(us),
        name="attend",
    )(*args)


def mix_kernel(o_ref, gate_ref, hp_ref, present_ref, wf_ref, m1_ref, x2_ref):
    pieces = []
    wf = wf_ref[...]
    for s in range(8):
        ot = jnp.concatenate([o_ref[h, s * 32 : (s + 1) * 32, :] for h in range(HEADS)], 0)
        at = (ot.astype(F32) * gate_ref[:, s * 128 : (s + 1) * 128]).astype(BF16)
        m1 = hp_ref[s].astype(F32) + dot_tn(at, wf)
        m1_ref[s] = m1
        pieces.append(standardize(m1).reshape(16, 8, 256))
    present = present_ref[...]
    wide = jnp.concatenate([present, jnp.zeros_like(present)], 1)
    pieces.append(jnp.stack([pltpu.roll(wide, (256 - 8 * a) % 256, 1) for a in range(16)], 0))
    x2_ref[...] = jnp.concatenate(pieces, 1).astype(BF16)


def mix_call(o, gate, hp, present, wf):
    return pl.pallas_call(
        mix_kernel,
        out_shape=(
            jax.ShapeDtypeStruct((8, 128, 256), F32),
            jax.ShapeDtypeStruct((16, 72, 256), BF16),
        ),
        in_specs=[whole()] * 5,
        out_specs=(whole(), whole()),
        compiler_params=params(),
        cost_estimate=cost(5),
        name="row_mix",
    )(o, gate, hp, present, wf)


def column_kernel(x_ref, wq_ref, wk_ref, wv_ref, wg_ref, out_ref, rows0, rows1):
    x = x_ref[...].astype(F32)
    rows = (rows0, rows1)
    xs = x[:, :64, :].reshape(1024, 256)
    rows0[...] = xs[:, :128]
    rows1[...] = xs[:, 128:]
    masks = (x[:, 64:72, :128].reshape(128, 128) - 1.0) * MASK_SCALE
    cols = jnp.concatenate(
        [jnp.concatenate([r[pl.ds(i, 128, stride=8), :] for r in rows], 1) for i in range(8)], 0
    ).astype(BF16)
    scale = HEAD_DIM ** (-0.5)
    qt = (dot_tt(wq_ref[...], cols) * scale).astype(BF16)
    kn = dot_nn(cols, wk_ref[...]).astype(BF16)
    vt = dot_tt(wv_ref[...], cols).astype(BF16)
    gt = jax.nn.sigmoid(dot_tt(wg_ref[...], cols))

    def scores(i, pair):
        lanes = slice(i * 128, (i + 1) * 128)
        sides = []
        for h in (pair * 2, pair * 2 + 1):
            parts = [qt[h * 32 : (h + 1) * 32, lanes]]
            if h > 0:
                parts.insert(0, jnp.zeros((h * 32, 128), BF16))
            if h < HEADS - 1:
                parts.append(jnp.zeros(((HEADS - 1 - h) * 32, 128), BF16))
            sides.append(jnp.concatenate(parts, 0))
        q = jnp.concatenate(sides, 1)
        return dot_nn(kn[i * 128 : (i + 1) * 128, :], q) + masks[:, i : i + 1]

    def finish(i, pair, score):
        lanes = slice(i * 128, (i + 1) * 128)
        probs = jnp.exp(score - jnp.max(score, 0, keepdims=True))
        total = jnp.sum(probs, 0, keepdims=True)
        accum = dot_nn(vt[pair * 64 : (pair + 1) * 64, lanes], probs.astype(BF16)) / total
        return [accum[:32, :128], accum[32:, 128:]]

    items = [(i, pair) for i in range(8) for pair in range(HEADS // 2)]
    score = scores(*items[0])
    heads = []
    for n, (i, pair) in enumerate(items):
        upcoming = scores(*items[n + 1]) if n + 1 < len(items) else None
        heads += finish(i, pair, score)
        score = upcoming
        if pair == HEADS // 2 - 1:
            an = (jnp.concatenate(heads, 0) * gt[:, i * 128 : (i + 1) * 128]).T
            heads = []
            for k, r in enumerate(rows):
                r[pl.ds(i, 128, stride=8), :] = an[:, k * 128 : (k + 1) * 128]
    out_ref[...] = jnp.concatenate([r[...] for r in rows], 1).astype(BF16).reshape(16, 64, 256)


def column_call(x, wq, wk, wv, wg):
    return pl.pallas_call(
        column_kernel,
        out_shape=jax.ShapeDtypeStruct((16, 64, 256), BF16),
        in_specs=[whole()] * 5,
        out_specs=whole(),
        scratch_shapes=[pltpu.VMEM((1024, 128), F32)] * 2,
        compiler_params=params(),
        cost_estimate=cost(10),
        name="column",
    )(x, wq, wk, wv, wg)


def final_kernel(a_ref, m1_ref, wf_ref, ww_ref, wn_ref, out_ref):
    a = a_ref[...].astype(F32)
    wf = wf_ref[...]
    ww = ww_ref[...]
    wn = wn_ref[...]
    for p in range(2):
        a2 = jnp.concatenate(
            [a[:, s * 8 : (s + 1) * 8, :].reshape(128, 256) for s in range(p * 4, p * 4 + 4)], 0
        ).astype(BF16)
        m2 = m1_ref[p * 4 : p * 4 + 4].reshape(512, 256) + dot_nn(a2, wf)
        x3 = standardize(m2).astype(BF16)
        hid = jnp.maximum(dot_nn(x3, ww), 0.0).astype(BF16)
        out_ref[p * 4 : p * 4 + 4] = (m2 + dot_nn(hid, wn)).astype(BF16).reshape(4, 128, 256)


def final_call(a, m1, wf, ww, wn):
    return pl.pallas_call(
        final_kernel,
        out_shape=jax.ShapeDtypeStruct((8, 128, 256), BF16),
        in_specs=[whole()] * 5,
        out_specs=whole(),
        compiler_params=params(),
        cost_estimate=cost(6),
        name="transition",
    )(a, m1, wf, ww, wn)


def on_device(
    homolog_profile,
    couplings_tensor,
    present_entries,
    resolved_positions,
    coupling_logit_matrix,
    horizontal_asking_matrix,
    horizontal_lookup_matrix,
    horizontal_content_matrix,
    horizontal_sigmoid_matrix,
    horizontal_final_matrix,
    vertical_asking_matrix,
    vertical_lookup_matrix,
    vertical_content_matrix,
    vertical_sigmoid_matrix,
    vertical_final_matrix,
    widening_matrix,
    narrowing_matrix,
):
    seq = lax.axis_index("seq")
    res = lax.axis_index("res")
    same_core = [[r for r in range(16) if r % 2 == c] for c in range(2)]
    to_right = [(a, (a + 2) % 16) for a in range(16)]
    to_left = [(a, (a - 2) % 16) for a in range(16)]
    swap = [(a, a ^ 1) for a in range(16)]

    wide_groups = [
        [(z * 2 + y) * 16 + g * 2 + c for y in range(2) for g in range(8)] for z in range(8) for c in range(2)
    ]

    def to_heads(x):
        return lax.all_to_all(x, "res", 0, 0, axis_index_groups=same_core, tiled=True)

    present = present_entries.astype(F32)
    okay = (present_entries * resolved_positions[None, :]).astype(F32)
    place = jnp.stack([seq // 2, res % 2]).astype(jnp.int32)

    barrier = lax.optimization_barrier
    bias = bias_call(couplings_tensor, coupling_logit_matrix.T)
    pair = lax.all_to_all(bias, ("seq", "res"), 0, 0, axis_index_groups=wide_groups, tiled=True)
    pair = pair.reshape(2, 8, 128, 128)
    send, gate = tokens_call(
        homolog_profile,
        okay,
        horizontal_asking_matrix,
        horizontal_lookup_matrix,
        horizontal_content_matrix,
        horizontal_sigmoid_matrix,
    )

    pair, send = barrier((pair, send))

    def ring(right, left):
        return lax.ppermute(right, "seq", to_right), lax.ppermute(left, "seq", to_left)

    def steps(far, *counts):
        blocks = []
        for n, k in counts:
            blocks += [(k, far, (n, n))] if k == 0 else [(-k, far, (n, n)), (k, far, (n + 1, n + 1))]
        return blocks

    one = ring(pair, pair)
    own = to_heads(send)
    two = ring(*one)
    own, one = barrier((own, one))
    other = lax.ppermute(own, "res", swap)
    near = [pair, *one]
    state = attend_call(place, own, None, near, steps(0, (0, 0), (1, 1)), None, False, 6)
    other, state = barrier((other, state))
    *state, other = attend_call(place, own, other, near, steps(1, (0, 0), (1, 1)), state, False, 6, True)
    two, state = barrier((two, state))
    three = ring(*two)
    state = attend_call(place, own, other, two, steps(0, (0, 2)) + steps(1, (0, 2)), state, False, 7)
    three, state = barrier((three, state))
    four = ring(three[0][:, :4], three[1][:, 4:])
    state = attend_call(place, own, other, three, steps(0, (0, 3)) + steps(1, (0, 3)), state, False, 7)
    o = attend_call(place, own, other, four, [(4, 0, (0, 1)), (4, 1, (0, 1))], state, True, 4)

    o = to_heads(o)
    m1, x2 = mix_call(o, gate, homolog_profile, present, horizontal_final_matrix)
    x2 = lax.all_to_all(x2, "seq", 0, 0, tiled=True)
    a2 = column_call(
        x2, vertical_asking_matrix, vertical_lookup_matrix, vertical_content_matrix, vertical_sigmoid_matrix
    )
    a2 = lax.all_to_all(a2, "seq", 0, 0, tiled=True)
    return final_call(a2, m1, vertical_final_matrix, widening_matrix, narrowing_matrix)


def solution(mesh):
    placed = (
        P("seq", "res", None),
        P("res", "seq", None),
        P("seq", "res"),
        P("res"),
    ) + (P(),) * 13
    return jax.shard_map(
        on_device, mesh=mesh, in_specs=placed, out_specs=P("seq", "res", None), check_vma=False
    )
```

```python
import functools

import jax
import jax.numpy as jnp
import numpy as np
from jax import lax
from jax.experimental import pallas as pl
from jax.experimental.pallas import tpu as pltpu
from jax.sharding import PartitionSpec as P

HEADS = 8
HEAD_DIM = 32
EPS = 1e-05
MASK_SCALE = 1000000000.0

F32 = jnp.float32
BF16 = jnp.bfloat16


def mask_parts():
    parts = []
    rest = np.float64(-MASK_SCALE)
    for _ in range(3):
        part = np.float64(np.asarray(rest, jnp.bfloat16))
        parts.append(float(part))
        rest = rest - part
    assert rest == 0.0
    return parts


def standardize(values):
    center = values - jnp.mean(values, -1, keepdims=True)
    spread = jnp.mean(center * center, -1, keepdims=True)
    return center * lax.rsqrt(spread + EPS)


def dot_tt(a, b):
    return lax.dot_general(a, b, (((0,), (1,)), ((), ())), preferred_element_type=F32)


def dot_tn(a, b):
    return lax.dot_general(a, b, (((0,), (0,)), ((), ())), preferred_element_type=F32)


def dot_nt(a, b):
    return lax.dot_general(a, b, (((1,), (1,)), ((), ())), preferred_element_type=F32)


def dot_nn(a, b):
    return lax.dot_general(a, b, (((1,), (0,)), ((), ())), preferred_element_type=F32)


def whole(*_):
    return pl.BlockSpec(memory_space=pltpu.VMEM)


def params(mib=24):
    return pltpu.CompilerParams(vmem_limit_bytes=mib * 1024 * 1024)


def cost(us):
    return pl.CostEstimate(flops=int(us * 1e-6 * 9e14), bytes_accessed=1024, transcendentals=0)


def tokens_kernel(hp_ref, ok_ref, wq_ref, wk_ref, wv_ref, wg_ref, send_ref, gate_ref):
    x = standardize(hp_ref[...].reshape(1024, 256).astype(F32)).astype(BF16)
    scale = HEAD_DIM ** (-0.5)
    for n, w_ref in enumerate((wq_ref, wk_ref, wv_ref)):
        t = dot_tt(w_ref[...], x)
        if n == 0:
            t = t * scale
        t = t.astype(BF16)
        for h in range(HEADS):
            for s in range(8):
                send_ref[h, n * 256 + s * 32 : n * 256 + (s + 1) * 32, :] = t[
                    h * 32 : (h + 1) * 32, s * 128 : (s + 1) * 128
                ]
    ok = jnp.concatenate([ok_ref[...], jnp.zeros((8, 128), F32)], 0).astype(BF16)
    for h in range(HEADS):
        send_ref[h, 768:784, :] = ok
    gate_ref[...] = jax.nn.sigmoid(dot_tt(wg_ref[...], x))


def tokens_call(hp, ok, wq, wk, wv, wg):
    return pl.pallas_call(
        tokens_kernel,
        out_shape=(
            jax.ShapeDtypeStruct((8, 784, 128), BF16),
            jax.ShapeDtypeStruct((256, 1024), F32),
        ),
        in_specs=[whole()] * 6,
        out_specs=(whole(), whole()),
        compiler_params=params(),
        cost_estimate=cost(5),
        name="tokens",
    )(hp, ok, wq, wk, wv, wg)


BIAS_ROWS = 64


def bias_kernel(z_ref, w_ref, out_ref, rows):
    step = pl.program_id(0)
    w = w_ref[...].astype(F32)
    wsum = jnp.sum(w, -1, keepdims=True)
    wt = jnp.concatenate([w, jnp.zeros((8, 128), F32)], 0).astype(BF16)
    for n in range(BIAS_ROWS):
        zt = z_ref[n].T
        zf = zt.astype(F32)
        mean = jnp.sum(zf, 0, keepdims=True) * (1.0 / 128)
        center = zf - mean
        spread = jnp.sum(center * center, 0, keepdims=True) * (1.0 / 128)
        res = (dot_nn(wt, zt)[0:8] - mean * wsum) * lax.rsqrt(spread + EPS)
        rows[pl.ds(step * BIAS_ROWS + n, 8, stride=128), :] = res

    @pl.when(step == pl.num_programs(0) - 1)
    def _():
        for h in range(HEADS):
            block = rows[h * 128 : (h + 1) * 128, :].T.astype(BF16)
            out_ref[h] = block
            out_ref[HEADS + h] = block


def bias_call(z, w):
    return pl.pallas_call(
        bias_kernel,
        out_shape=jax.ShapeDtypeStruct((16, 128, 128), BF16),
        grid=(128 // BIAS_ROWS,),
        in_specs=[
            pl.BlockSpec((BIAS_ROWS, 128, 128), lambda n: (n, 0, 0)),
            pl.BlockSpec((8, 128), lambda n: (0, 0)),
        ],
        out_specs=pl.BlockSpec((16, 128, 128), lambda n: (0, 0, 0)),
        scratch_shapes=[pltpu.VMEM((1024, 128), F32)],
        compiler_params=params(60),
        cost_estimate=cost(6),
        name="pair_bias",
    )(z, w)


def attend_kernel(width, unroll, n_bias, blocks, has_other, fetch, first, last, *refs):
    place_ref, own_ref = refs[:2]
    refs = refs[2:]
    if has_other:
        far_ref, refs = refs[0], refs[1:]
    bias_refs = refs[:n_bias]
    refs = refs[n_bias:]
    if not first:
        m_in, l_in, acc_in = refs[:3]
        refs = refs[3:]
    copy = None
    if fetch:
        other_ref, far_ref, sem = far_ref, refs[3], refs[5]
        refs = [*refs[:3], refs[4]]
        copy = pltpu.make_async_copy(other_ref.at[:, pl.ds(256, 528)], far_ref, sem)
        copy.start()
    if last:
        o_ref, keys = refs
    else:
        m_ref, l_ref, acc_ref, keys = refs
    z = place_ref[0]
    core = place_ref[1]
    parts = mask_parts()
    rowid = lax.broadcasted_iota(jnp.int32, (16, 128), 0)
    coeff = jnp.where(rowid == 0, parts[0], jnp.where(rowid == 1, parts[1], jnp.where(rowid == 2, parts[2], 0.0)))
    rowid = lax.broadcasted_iota(jnp.int32, (16, width), 0)
    ones = jnp.where(rowid < 3, 1.0, 0.0).astype(BF16)
    places = []
    for shift, far, _ in blocks:
        zz = lax.rem(z + shift + 8, 8)
        places.append((far_ref, zz, 0) if far else (own_ref, zz, 256))

    if copy is not None:
        copy.wait()
    for n, (src, at, base) in enumerate(places):
        okay = src[at, base + 512 : base + 528, :].astype(F32)
        for s in range(8):
            mask = ((1.0 - okay[s : s + 1, :]) * coeff).astype(BF16)
            keys[n, s] = jnp.concatenate([src[at, base + s * 32 : base + (s + 1) * 32, :], mask], 0).T

    span = width // 128

    def bias_block(n, tile):
        _, far, operands = blocks[n]
        slot = 1 - core if far else core
        ref = bias_refs[operands[tile * width // 512]]
        base = tile * span if ref.shape[1] == 8 else tile * span % 4
        return jnp.concatenate([ref[slot, base + u] for u in range(span)], 1)

    def scores(s, tile):
        kx = jnp.concatenate([keys[n, s] for n in range(len(blocks))], 0)
        q = jnp.concatenate(
            [own_ref[tile * span + u, pl.ds(pl.multiple_of(s * 32, 32), 32), :] for u in range(span)], 1
        )
        qx = jnp.concatenate([q, ones], 0)
        bias = jnp.concatenate([bias_block(n, tile) for n in range(len(blocks))], 0)
        return dot_nn(kx, qx) + bias.astype(F32)

    def finish(s, tile, score):
        lanes = slice(tile * width, (tile + 1) * width)
        top = jnp.max(score, 0, keepdims=True)
        if not first:
            before = m_in[s, :, lanes]
            top = jnp.maximum(top, before)
        probs = jnp.exp(score - top)
        total = jnp.sum(probs, 0, keepdims=True)
        vt = jnp.concatenate(
            [src[at, pl.ds(pl.multiple_of(base + 256 + s * 32, 32), 32), :] for src, at, base in places], 1
        )
        accum = dot_nn(vt, probs.astype(BF16))
        if not first:
            factor = jnp.exp(before - top)
            total = total + l_in[s, :, lanes] * factor
            accum = accum + acc_in[s, :, lanes] * factor
        if last:
            out = (accum / total).astype(o_ref.dtype)
            for u in range(span):
                o_ref[tile * span + u, pl.ds(pl.multiple_of(s * 32, 32), 32), :] = out[
                    :, u * 128 : (u + 1) * 128
                ]
        else:
            m_ref[s, :, lanes] = top
            l_ref[s, :, lanes] = total
            acc_ref[s, :, lanes] = accum

    def some_sequences(k, carry):
        items = [(k * unroll + d, tile) for d in range(unroll) for tile in range(1024 // width)]
        score = scores(*items[0])
        for n, item in enumerate(items):
            upcoming = scores(*items[n + 1]) if n + 1 < len(items) else None
            finish(*item, score)
            score = upcoming
        return carry

    lax.fori_loop(0, 8 // unroll, some_sequences, 0)


def attend_call(place, own, other, biases, blocks, state, last, us, fetch=False):
    first = state is None
    if last:
        out_shape = jax.ShapeDtypeStruct((8, 256, 128), F32)
        out_specs = whole()
    else:
        out_shape = (
            jax.ShapeDtypeStruct((8, 1, 1024), F32),
            jax.ShapeDtypeStruct((8, 1, 1024), F32),
            jax.ShapeDtypeStruct((8, 32, 1024), F32),
        )
        out_specs = (whole(),) * 3
    args = [place, own] + ([] if other is None else [other]) + list(biases) + ([] if first else list(state))
    in_specs = [pl.BlockSpec(memory_space=pltpu.SMEM)] + [whole()] * (len(args) - 1)
    scratch = [pltpu.VMEM((len(blocks), 8, 128, 48), BF16)]
    if fetch:
        in_specs[2] = pl.BlockSpec(memory_space=pl.ANY)
        out_shape += (jax.ShapeDtypeStruct((8, 528, 128), BF16),)
        out_specs += (whole(),)
        scratch.append(pltpu.SemaphoreType.DMA)
    unroll = 4 if len(blocks) <= 4 else 2
    return pl.pallas_call(
        functools.partial(attend_kernel, 512, unroll, len(biases), blocks, other is not None, fetch, first, last),
        out_shape=out_shape,
        in_specs=in_specs,
        out_specs=out_specs,
        scratch_shapes=scratch,
        compiler_params=params(),
        cost_estimate=cost(us),
        name="attend",
    )(*args)


def mix_kernel(o_ref, gate_ref, hp_ref, present_ref, wf_ref, m1_ref, x2_ref):
    pieces = []
    wf = wf_ref[...]
    for s in range(8):
        ot = jnp.concatenate([o_ref[h, s * 32 : (s + 1) * 32, :] for h in range(HEADS)], 0)
        at = (ot.astype(F32) * gate_ref[:, s * 128 : (s + 1) * 128]).astype(BF16)
        m1 = hp_ref[s].astype(F32) + dot_tn(at, wf)
        m1_ref[s] = m1
        pieces.append(standardize(m1).reshape(16, 8, 256))
    present = present_ref[...]
    wide = jnp.concatenate([present, jnp.zeros_like(present)], 1)
    pieces.append(jnp.stack([pltpu.roll(wide, (256 - 8 * a) % 256, 1) for a in range(16)], 0))
    x2_ref[...] = jnp.concatenate(pieces, 1).astype(BF16)


def mix_call(o, gate, hp, present, wf):
    return pl.pallas_call(
        mix_kernel,
        out_shape=(
            jax.ShapeDtypeStruct((8, 128, 256), F32),
            jax.ShapeDtypeStruct((16, 72, 256), BF16),
        ),
        in_specs=[whole()] * 5,
        out_specs=(whole(), whole()),
        compiler_params=params(),
        cost_estimate=cost(5),
        name="row_mix",
    )(o, gate, hp, present, wf)


def column_kernel(x_ref, wq_ref, wk_ref, wv_ref, wg_ref, out_ref, rows0, rows1):
    x = x_ref[...].astype(F32)
    rows = (rows0, rows1)
    xs = x[:, :64, :].reshape(1024, 256)
    rows0[...] = xs[:, :128]
    rows1[...] = xs[:, 128:]
    masks = (x[:, 64:72, :128].reshape(128, 128) - 1.0) * MASK_SCALE
    cols = jnp.concatenate(
        [jnp.concatenate([r[pl.ds(i, 128, stride=8), :] for r in rows], 1) for i in range(8)], 0
    ).astype(BF16)
    scale = HEAD_DIM ** (-0.5)
    qt = (dot_tt(wq_ref[...], cols) * scale).astype(BF16)
    kn = dot_nn(cols, wk_ref[...]).astype(BF16)
    vt = dot_tt(wv_ref[...], cols).astype(BF16)
    gt = jax.nn.sigmoid(dot_tt(wg_ref[...], cols))

    def scores(i, pair):
        lanes = slice(i * 128, (i + 1) * 128)
        sides = []
        for h in (pair * 2, pair * 2 + 1):
            parts = [qt[h * 32 : (h + 1) * 32, lanes]]
            if h > 0:
                parts.insert(0, jnp.zeros((h * 32, 128), BF16))
            if h < HEADS - 1:
                parts.append(jnp.zeros(((HEADS - 1 - h) * 32, 128), BF16))
            sides.append(jnp.concatenate(parts, 0))
        q = jnp.concatenate(sides, 1)
        return dot_nn(kn[i * 128 : (i + 1) * 128, :], q) + masks[:, i : i + 1]

    def finish(i, pair, score):
        lanes = slice(i * 128, (i + 1) * 128)
        probs = jnp.exp(score - jnp.max(score, 0, keepdims=True))
        total = jnp.sum(probs, 0, keepdims=True)
        accum = dot_nn(vt[pair * 64 : (pair + 1) * 64, lanes], probs.astype(BF16)) / total
        return [accum[:32, :128], accum[32:, 128:]]

    items = [(i, pair) for i in range(8) for pair in range(HEADS // 2)]
    score = scores(*items[0])
    heads = []
    for n, (i, pair) in enumerate(items):
        upcoming = scores(*items[n + 1]) if n + 1 < len(items) else None
        heads += finish(i, pair, score)
        score = upcoming
        if pair == HEADS // 2 - 1:
            an = (jnp.concatenate(heads, 0) * gt[:, i * 128 : (i + 1) * 128]).T
            heads = []
            for k, r in enumerate(rows):
                r[pl.ds(i, 128, stride=8), :] = an[:, k * 128 : (k + 1) * 128]
    out_ref[...] = jnp.concatenate([r[...] for r in rows], 1).astype(BF16).reshape(16, 64, 256)


def column_call(x, wq, wk, wv, wg):
    return pl.pallas_call(
        column_kernel,
        out_shape=jax.ShapeDtypeStruct((16, 64, 256), BF16),
        in_specs=[whole()] * 5,
        out_specs=whole(),
        scratch_shapes=[pltpu.VMEM((1024, 128), F32)] * 2,
        compiler_params=params(),
        cost_estimate=cost(10),
        name="column",
    )(x, wq, wk, wv, wg)


def final_kernel(a_ref, m1_ref, wf_ref, ww_ref, wn_ref, out_ref, done, sems):
    a = a_ref[...].astype(F32)
    wf = wf_ref[...]
    ww = ww_ref[...]
    wn = wn_ref[...]

    def front(p):
        a2 = jnp.concatenate(
            [a[:, s * 8 : (s + 1) * 8, :].reshape(128, 256) for s in (p * 2, p * 2 + 1)], 0
        ).astype(BF16)
        m2 = m1_ref[p * 2 : p * 2 + 2].reshape(256, 256) + dot_nn(a2, wf)
        return m2, standardize(m2).astype(BF16)

    copies = []
    m2, x3 = front(0)
    for p in range(4):
        upcoming = front(p + 1) if p < 3 else (None, None)
        hid = jnp.maximum(dot_nn(x3, ww), 0.0).astype(BF16)
        done[p * 2 : p * 2 + 2] = (m2 + dot_nn(hid, wn)).astype(BF16).reshape(2, 128, 256)
        copies.append(
            pltpu.make_async_copy(done.at[pl.ds(p * 2, 2)], out_ref.at[pl.ds(p * 2, 2)], sems.at[p])
        )
        copies[-1].start()
        m2, x3 = upcoming
    for copy in copies:
        copy.wait()


def final_call(a, m1, wf, ww, wn):
    return pl.pallas_call(
        final_kernel,
        out_shape=jax.ShapeDtypeStruct((8, 128, 256), BF16),
        in_specs=[whole()] * 5,
        out_specs=pl.BlockSpec(memory_space=pl.ANY),
        scratch_shapes=[pltpu.VMEM((8, 128, 256), BF16), pltpu.SemaphoreType.DMA((4,))],
        compiler_params=params(),
        cost_estimate=cost(4),
        name="transition",
    )(a, m1, wf, ww, wn)


def on_device(
    homolog_profile,
    couplings_tensor,
    present_entries,
    resolved_positions,
    coupling_logit_matrix,
    horizontal_asking_matrix,
    horizontal_lookup_matrix,
    horizontal_content_matrix,
    horizontal_sigmoid_matrix,
    horizontal_final_matrix,
    vertical_asking_matrix,
    vertical_lookup_matrix,
    vertical_content_matrix,
    vertical_sigmoid_matrix,
    vertical_final_matrix,
    widening_matrix,
    narrowing_matrix,
):
    seq = lax.axis_index("seq")
    res = lax.axis_index("res")
    same_core = [[r for r in range(16) if r % 2 == c] for c in range(2)]
    to_right = [(a, (a + 2) % 16) for a in range(16)]
    to_left = [(a, (a - 2) % 16) for a in range(16)]
    swap = [(a, a ^ 1) for a in range(16)]

    wide_groups = [
        [(z * 2 + y) * 16 + g * 2 + c for y in range(2) for g in range(8)] for z in range(8) for c in range(2)
    ]

    def to_heads(x):
        return lax.all_to_all(x, "res", 0, 0, axis_index_groups=same_core, tiled=True)

    present = present_entries.astype(F32)
    okay = (present_entries * resolved_positions[None, :]).astype(F32)
    place = jnp.stack([seq // 2, res % 2]).astype(jnp.int32)

    barrier = lax.optimization_barrier
    bias = bias_call(couplings_tensor, coupling_logit_matrix.T)
    pair = lax.all_to_all(bias, ("seq", "res"), 0, 0, axis_index_groups=wide_groups, tiled=True)
    pair = pair.reshape(2, 8, 128, 128)
    send, gate = tokens_call(
        homolog_profile,
        okay,
        horizontal_asking_matrix,
        horizontal_lookup_matrix,
        horizontal_content_matrix,
        horizontal_sigmoid_matrix,
    )

    pair, send = barrier((pair, send))

    def ring(right, left):
        return lax.ppermute(right, "seq", to_right), lax.ppermute(left, "seq", to_left)

    def steps(far, *counts):
        blocks = []
        for n, k in counts:
            blocks += [(k, far, (n, n))] if k == 0 else [(-k, far, (n, n)), (k, far, (n + 1, n + 1))]
        return blocks

    one = ring(pair, pair)
    own = to_heads(send)
    two = ring(*one)
    own, one = barrier((own, one))
    other = lax.ppermute(own, "res", swap)
    near = [pair, *one]
    state = attend_call(place, own, None, near, steps(0, (0, 0), (1, 1)), None, False, 6)
    other, state = barrier((other, state))
    *state, other = attend_call(place, own, other, near, steps(1, (0, 0), (1, 1)), state, False, 6, True)
    two, state = barrier((two, state))
    three = ring(*two)
    state = attend_call(place, own, other, two, steps(0, (0, 2)) + steps(1, (0, 2)), state, False, 7)
    three, state = barrier((three, state))
    four = ring(three[0][:, :4], three[1][:, 4:])
    state = attend_call(place, own, other, three, steps(0, (0, 3)) + steps(1, (0, 3)), state, False, 7)
    o = attend_call(place, own, other, four, [(4, 0, (0, 1)), (4, 1, (0, 1))], state, True, 4)

    o = to_heads(o)
    m1, x2 = mix_call(o, gate, homolog_profile, present, horizontal_final_matrix)
    x2 = lax.all_to_all(x2, "seq", 0, 0, tiled=True)
    a2 = column_call(
        x2, vertical_asking_matrix, vertical_lookup_matrix, vertical_content_matrix, vertical_sigmoid_matrix
    )
    a2 = lax.all_to_all(a2, "seq", 0, 0, tiled=True)
    return final_call(a2, m1, vertical_final_matrix, widening_matrix, narrowing_matrix)


def solution(mesh):
    placed = (
        P("seq", "res", None),
        P("res", "seq", None),
        P("seq", "res"),
        P("res"),
    ) + (P(),) * 13
    return jax.shard_map(
        on_device, mesh=mesh, in_specs=placed, out_specs=P("seq", "res", None), check_vma=False
    )
```
